128 devices in a mesh: seq: 16 (over z, x), head: 8 (over y, core).
Axes of the slice: x: 4, y: 4, z: 4, core: 2. Of those that a mesh axis runs over, the one named last changes fastest.
Arguments:
- tokens: bfloat16 [8192, 3072], P(('seq', 'head')), may hold values from -6 to 6
- block_target: int32 [512], replicated, may hold values from 0 to 15, as said below
- clip_within: int32 [512], replicated, may hold values from 0 to 3, as said below
- modulation: float32 [64, 3, 3072], P('seq'), may hold values from -6 to 6
- inner_attention: bfloat16 [3072, 3, 2048], P(None, None, 'head'), may hold values from -0.109375 to 0.109375
- inner_hidden: bfloat16 [3072, 6144], P(None, 'head'), may hold values from -0.109375 to 0.109375
- outer_attention: bfloat16 [2048, 3072], P('head'), may hold values from -0.125 to 0.125
- outer_hidden: bfloat16 [6144, 3072], P('head'), may hold values from -0.078125 to 0.078125
Outputs:
- mixed_tokens: bfloat16 [8192, 3072], P(('seq', 'head'))
The draws below stay inside these ranges and needn't reach their ends.
Inputs may be any that keep to these rules, and one draw needn't show every extreme that they name: `block_target`: the 4 blocks of one device go to different seq indices. Counting only the devices of one head index, each seq index receives 2 to 6 blocks, and some seq index receives exactly 6 of them. `clip_within`: blocks with the same target and the same number form one clip; at each seq index the numbers never fall along the block order, and its first block has number 0 and its last 3.
All inputs are finite; a program needn't handle non-finite values.
Results may differ from the reference program's by a relative error of at most 0.017.
Values may be sent and summed in bfloat16 or wider, within the bound.
A program may use at most 128 MiB of HBM per device.

```python
from functools import partial
import jax
import jax.numpy as jnp
from jax import lax

D = 3072
HEADS = 16
HD = 128
HID = 6144
BLOCK = 16
BLK_DEV = 4
CPG = 4
RCAP = 6
NBLK = 512
TOKENS = 8192
NCLIP = 64
N_HEAD = 8


def head_table(key, seq_total):
    key_delta, key_order, key_rows = jax.random.split(key, 3)
    delta = jax.random.randint(key_delta, (seq_total // 2,), 0, 3)
    delta = delta.at[0].set(2)
    loads = jnp.stack([BLK_DEV + delta, BLK_DEV - delta], axis=1).reshape(seq_total)
    loads = loads[jax.random.permutation(key_order, seq_total)]
    ends = jnp.cumsum(loads)
    places = jnp.arange(seq_total * BLK_DEV)
    runs = jnp.sum((places[:, None] >= ends[None, :]).astype(jnp.int32), axis=1)
    table = runs.reshape(BLK_DEV, seq_total).T
    return table[jax.random.permutation(key_rows, seq_total)]


def draw_routes(key):
    seq_total = NCLIP // CPG
    head_total = NBLK // (seq_total * BLK_DEV)
    key_tables, key_cuts = jax.random.split(jax.random.fold_in(key, 11))
    tables = jax.vmap(partial(head_table, seq_total=seq_total))(jax.random.split(key_tables, head_total))
    target = jnp.transpose(tables, (1, 0, 2)).reshape(NBLK).astype(jnp.int32)
    member = (target[:, None] == jnp.arange(seq_total, dtype=jnp.int32)[None, :]).astype(jnp.int32)
    before = jnp.cumsum(member, axis=0) - member
    place = jnp.sum(before * member, axis=1)
    counts = jnp.sum(member, axis=0)
    cuts = jax.random.randint(key_cuts, (seq_total, CPG - 1), 1, jnp.maximum(counts, 2)[:, None])
    within = jnp.sum((place[:, None] >= cuts[target]).astype(jnp.int32), axis=1)
    return (target, within.astype(jnp.int32))


def draw_block_target(key, part):
    shared = draw_routes(key)
    return shared[0]


def draw_clip_within(key, part):
    shared = draw_routes(key)
    return shared[1]


def levels(rng, shape, cuts, least, largest):
    gain, own = 1.0, jax.random.fold_in(rng, 6)
    for position, shards_of in cuts:
        heights = jnp.exp(jax.random.uniform(jax.random.fold_in(own, position), (shards_of,), jnp.float32, least / len(cuts), largest / len(cuts)))
        gain = gain * jnp.repeat(heights, shape[position] // shards_of).reshape([-1 if axis == position else 1 for axis in range(len(shape))])
    return gain


def noise(key, extent, scale, limit, shards=(), kind=jnp.bfloat16):
    entries = jax.random.normal(key, extent, jnp.float32) * scale
    if len(shards) > 0:
        entries = levels(key, extent, shards, -0.22, 0.18) * entries
    return jnp.clip(entries, min=-limit, max=limit).astype(kind)


def setup_inputs(seed: int = 0) -> dict:
    key_of = jax.random.split(jax.random.key(seed), 9)
    return {
        "tokens": noise(key_of[0], (TOKENS, D), 1.0, 6.0, ((0, 128),)),
        "block_target": draw_block_target(jax.random.fold_in(key_of[8], 71), 0),
        "clip_within": draw_clip_within(jax.random.fold_in(key_of[8], 71), 0),
        "modulation": noise(key_of[3], (NCLIP, 3, D), 1.0, 6.0, ((0, 16),), jnp.float32),
        "inner_attention": noise(key_of[4], (D, 3, HEADS * HD), D ** -0.5, 0.109375, ((2, 8),)),
        "inner_hidden": noise(key_of[5], (D, HID), D ** -0.5, 0.109375, ((1, 8),)),
        "outer_attention": noise(key_of[6], (HEADS * HD, D), (HEADS * HD) ** -0.5, 0.125, ((0, 8),)),
        "outer_hidden": noise(key_of[7], (HID, D), HID ** -0.5, 0.078125, ((0, 8),)),
    }


EPSILON = 1e-06

def layer_norm(values):
    centred = values - lax.optimization_barrier(jnp.mean(values, axis=-1, keepdims=True))
    return centred * lax.rsqrt(lax.optimization_barrier(jnp.mean(centred * centred, axis=-1, keepdims=True)) + EPSILON)

def rms_norm(values):
    return values * lax.rsqrt(lax.optimization_barrier(jnp.mean(values * values, axis=-1, keepdims=True)) + EPSILON)

def reference(tokens, block_target, clip_within, modulation, inner_attention, inner_hidden, outer_attention, outer_hidden):
    seq_total = NCLIP // CPG
    slots = N_HEAD * RCAP
    clip_ids = (block_target * CPG + clip_within).astype(jnp.int32)
    blocks = tokens.astype(jnp.float32).reshape(NBLK, BLOCK, D)
    picked = modulation[clip_ids]
    shaped = layer_norm(blocks) * (1.0 + picked[:, 1][:, None, :]) + picked[:, 0][:, None, :]
    modulated = shaped.astype(jnp.bfloat16).reshape(TOKENS, D)
    projected = jnp.dot(modulated, inner_attention.reshape(D, 3 * HEADS * HD), preferred_element_type=jnp.float32)
    projected = projected.reshape(TOKENS, 3, HEADS, HD)
    queries = rms_norm(projected[:, 0]).astype(jnp.bfloat16)
    keys_all = rms_norm(projected[:, 1]).astype(jnp.bfloat16)
    values_all = projected[:, 2].astype(jnp.bfloat16)
    hidden = jax.nn.gelu(jnp.dot(modulated, inner_hidden, preferred_element_type=jnp.float32), approximate=True).astype(jnp.bfloat16)
    order = jnp.argsort(block_target, stable=True).astype(jnp.int32)
    counts = lax.optimization_barrier(jnp.sum((block_target[:, None] == jnp.arange(seq_total, dtype=jnp.int32)[None, :]).astype(jnp.int32), axis=0))
    starts = (jnp.cumsum(counts) - counts).astype(jnp.int32)
    offsets = jnp.arange(slots, dtype=jnp.int32)
    positions = jnp.minimum(starts[:, None] + offsets[None, :], NBLK - 1).astype(jnp.int32)
    chosen_all = jnp.where(offsets[None, :] < counts[:, None], order[positions], NBLK).astype(jnp.int32)
    pad_shape = (1, BLOCK, HEADS, HD)
    query_pad = jnp.concatenate([queries.reshape(NBLK, BLOCK, HEADS, HD), jnp.zeros(pad_shape, jnp.bfloat16)], axis=0)
    key_pad = jnp.concatenate([keys_all.reshape(NBLK, BLOCK, HEADS, HD), jnp.zeros(pad_shape, jnp.bfloat16)], axis=0)
    value_pad = jnp.concatenate([values_all.reshape(NBLK, BLOCK, HEADS, HD), jnp.zeros(pad_shape, jnp.bfloat16)], axis=0)
    clip_pad = jnp.concatenate([clip_ids, jnp.full((1,), -1, jnp.int32)], axis=0)
    scale = HD ** (-0.5)

    def one_group(chosen):
        query = jnp.take(query_pad, chosen, axis=0).reshape(slots * BLOCK, HEADS, HD).astype(jnp.float32)
        key_rows = jnp.take(key_pad, chosen, axis=0).reshape(slots * BLOCK, HEADS, HD).astype(jnp.float32)
        value_rows = jnp.take(value_pad, chosen, axis=0).reshape(slots * BLOCK, HEADS, HD).astype(jnp.float32)
        token_clip = jnp.repeat(jnp.take(clip_pad, chosen, axis=0), BLOCK)
        scores = jnp.einsum('qhd,khd->hqk', query, key_rows) * scale
        mask = token_clip[:, None] == token_clip[None, :]
        powers = jnp.where(mask[None], jnp.exp(scores), 0.0)
        weights = (powers / lax.optimization_barrier(jnp.sum(powers, axis=-1, keepdims=True))).astype(jnp.bfloat16)
        mixed = jnp.einsum('hqk,khd->qhd', weights.astype(jnp.float32), value_rows)
        return mixed.astype(jnp.bfloat16).reshape(slots, BLOCK, HEADS * HD)
    grouped = lax.map(one_group, chosen_all)
    attended = jnp.zeros((NBLK + 1, BLOCK, HEADS * HD), jnp.bfloat16)
    attended = attended.at[chosen_all.reshape(-1)].set(grouped.reshape(seq_total * slots, BLOCK, HEADS * HD))
    attended = attended[:NBLK].reshape(TOKENS, HEADS * HD)
    share_att = HEADS * HD // N_HEAD
    share_hid = HID // N_HEAD

    def add_share(share, total):
        index = jnp.asarray(share).astype(jnp.int32)
        left_att = lax.dynamic_slice_in_dim(attended, index * share_att, share_att, 1)
        rows_att = lax.dynamic_slice_in_dim(outer_attention, index * share_att, share_att, 0)
        left_hid = lax.dynamic_slice_in_dim(hidden, index * share_hid, share_hid, 1)
        rows_hid = lax.dynamic_slice_in_dim(outer_hidden, index * share_hid, share_hid, 0)
        term = jnp.dot(left_att, rows_att, preferred_element_type=jnp.float32) + jnp.dot(left_hid, rows_hid, preferred_element_type=jnp.float32)
        rounded = lax.optimization_barrier(term.astype(jnp.bfloat16))
        return total + rounded.astype(jnp.float32)
    branch = lax.fori_loop(0, N_HEAD, add_share, jnp.zeros((TOKENS, D), jnp.float32))
    mixed_tokens = blocks + picked[:, 2][:, None, :] * branch.reshape(NBLK, BLOCK, D)
    return mixed_tokens.astype(jnp.bfloat16).reshape(TOKENS, D)
```

```python
import math

import jax
import jax.numpy as jnp
from jax import lax
from jax.experimental import pallas as pl
from jax.experimental.pallas import tpu as pltpu
from jax.sharding import PartitionSpec as P

MESH = pl.DeviceIdType.MESH
F32 = jnp.float32
BF16 = jnp.bfloat16

HD = 128
BLOCK = 16
BLK_DEV = 4
CPG = 4
RCAP = 6
EPSILON = 1e-06

Z = 4
X = 4
NSEQ = Z * X
Y = 4
NHEAD = 8
D = 3072
ROWS = RCAP * BLOCK
ALL = NHEAD * ROWS
HALF = ROWS // 2
NC = 4
CC = D // NC
TILE = 256
QT = 256
NT = CC // TILE
ATT = 256
HID = 768
BIG = 1536.0
EXP_A = HD ** (-0.5) * math.log2(math.e)
EXP_B = BIG * EXP_A

OFFSETS = sorted(
    [(a, b) for a in range(Z) for b in range(X) if (a, b) != (0, 0)],
    key=lambda o: -(min(o[0], Z - o[0]) + min(o[1], X - o[1])),
)


def kernel(
    bt, cw, tok, md, wq, wh, woa, woh, out,
    nrm, inbox, st_a, rv_a, gath, win, wo, acc, qa, ka, va, ah,
    term, rv_s, rv_f, rv_n, fin, st_e, rv_e, ranks, srcs, clips,
    w_sem, ss_a, rs_a, ss_b, rs_b, ss_g, rs_g,
    ss_s, rs_s, ss_f, rs_f, ss_n, rs_n, ss_e, rs_e,
):
    me = lax.axis_index("seq")
    head = lax.axis_index("head")
    z, x = me // X, me % X
    y, core = head // 2, head % 2
    sibling = head + 1 - 2 * core
    group = core * Y + y

    def seq_at(dz, dx):
        return ((z + dz) % Z) * X + (x + dx) % X

    def head_at(dy):
        return ((y + dy) % Y) * 2 + core

    def remote(src, dst, ss, rs, dev):
        return pltpu.make_async_remote_copy(
            src_ref=src, dst_ref=dst, send_sem=ss, recv_sem=rs, device_id=dev, device_id_type=MESH
        )

    loads = [
        pltpu.make_async_copy(wq, win.at[pl.ds(0, 3)], w_sem.at[0]),
        pltpu.make_async_copy(woa, wo.at[pl.ds(0, ATT)], w_sem.at[1]),
        pltpu.make_async_copy(woh, wo.at[pl.ds(ATT, HID)], w_sem.at[2]),
    ] + [
        pltpu.make_async_copy(wh.at[:, pl.ds(n * TILE, TILE)], win.at[3 + n], w_sem.at[3 + n])
        for n in range(3)
    ]
    for load in loads:
        load.start()

    barrier = pltpu.get_barrier_semaphore()
    for dz, dx in OFFSETS:
        pl.semaphore_signal(barrier, inc=1, device_id=(seq_at(dz, dx), head), device_id_type=MESH)
    for dy in range(1, Y):
        pl.semaphore_signal(barrier, inc=1, device_id=(me, head_at(dy)), device_id_type=MESH)
    pl.semaphore_signal(barrier, inc=1, device_id=(me, sibling), device_id_type=MESH)

    for j in range(BLK_DEV):
        rows = tok[j * BLOCK : (j + 1) * BLOCK, :].astype(F32)
        centred = rows - jnp.mean(rows, axis=-1, keepdims=True)
        scale = lax.rsqrt(jnp.mean(centred * centred, axis=-1, keepdims=True) + EPSILON)
        nrm[j] = (centred * scale).astype(BF16)
    base = (me * NHEAD + head) * BLK_DEV
    targets = [bt[base + j] for j in range(BLK_DEV)]

    def stage(t, carry):
        pick = jnp.int32(0)
        for j in range(1, BLK_DEV):
            pick = jnp.where(targets[j] == t, j, pick)
        block = nrm[pick]
        for c in range(NC):
            st_a[c, t] = block[:, c * CC : (c + 1) * CC]
        return carry

    lax.fori_loop(0, NSEQ, stage, 0)
    pl.semaphore_wait(barrier, NSEQ - 1 + Y)

    def send_a(c, k):
        to = seq_at(*OFFSETS[k])
        return remote(st_a.at[c, to], rv_a.at[c, me], ss_a.at[c, k], rs_a.at[c, k], (to, head))

    def got_a(c, k):
        dz, dx = OFFSETS[k]
        frm = seq_at(Z - dz, X - dx)
        return remote(st_a.at[c, frm], rv_a.at[c, frm], ss_a.at[c, k], rs_a.at[c, k], (frm, head))

    def start_a(c, carry):
        for k in range(NSEQ - 1):
            send_a(c, k).start()
        rv_a[c, me] = st_a[c, me]
        return carry

    lax.fori_loop(0, NC, start_a, 0)

    def entry(s, h):
        live, clip = jnp.int32(0), jnp.int32(0)
        for j in range(BLK_DEV):
            at = (s * NHEAD + h) * BLK_DEV + j
            hit = bt[at] == me
            live = jnp.where(hit, 1, live)
            clip = jnp.where(hit, cw[at], clip)
        return live, clip

    def own_slot(s, carry):
        count, picked, named = carry
        live, clip = entry(s, head)
        ranks[s] = jnp.minimum(count, RCAP - 1)
        at = jnp.where(live == 1, count, -1)
        picked = tuple(jnp.where(at == r, s, picked[r]) for r in range(RCAP))
        named = tuple(jnp.where(at == r, clip, named[r]) for r in range(RCAP))
        return count + live, picked, named

    zeros = (jnp.int32(0),) * RCAP
    _, picked, named = lax.fori_loop(0, NSEQ, own_slot, (jnp.int32(0), zeros, zeros))
    for r in range(RCAP):
        srcs[r] = picked[r]
        clips[r] = named[r]

    lanes = lax.broadcasted_iota(jnp.int32, (BLOCK, HD), 1)

    def group_slots(g, carry):
        h = (g % Y) * 2 + g // Y

        def slot(s, carry):
            count, named = carry
            live, clip = entry(s, h)
            at = jnp.where(live == 1, count, -1)
            return count + live, tuple(jnp.where(at == r, clip, named[r]) for r in range(RCAP))

        dead = (jnp.int32(CPG),) * RCAP
        _, named = lax.fori_loop(0, NSEQ, slot, (jnp.int32(0), dead))
        for r in range(RCAP):
            one = jnp.where(lanes == named[r], 1.0, 0.0)
            at = pl.ds(pl.multiple_of(g * ROWS + r * BLOCK, BLOCK), BLOCK)
            for i in range(2):
                qa[i, at, HD:] = (one * BIG).astype(BF16)
                ka[i, at, HD:] = one.astype(BF16)
                va[i, at, HD:] = jnp.ones((BLOCK, HD), BF16)
        return carry

    lax.fori_loop(0, NHEAD, group_slots, 0)

    def clear(n, carry):
        acc[n] = jnp.zeros((ALL, TILE), F32)
        return carry

    lax.fori_loop(0, 6, clear, 0)

    def own_rows(c):
        return gath.at[c, group]

    def rows_of(c, dy):
        return gath.at[c, core * Y + (y + dy) % Y]

    def rows_of_sibling(c, dy):
        return gath.at[c, (1 - core) * Y + (y + dy) % Y]

    def send_b(c, k):
        return remote(own_rows(c), own_rows(c), ss_b.at[c, k], rs_b.at[c, k], (me, head_at(k)))

    def got_b(c, k):
        ref = rows_of(c, Y - k)
        return remote(ref, ref, ss_b.at[c, k], rs_b.at[c, k], (me, head_at(Y - k)))

    def send_g(c, k):
        ref = rows_of(c, Y - k)
        return remote(ref, ref, ss_g.at[c, k], rs_g.at[c, k], (me, sibling))

    def got_g(c, k):
        ref = rows_of_sibling(c, Y - k)
        return remote(ref, ref, ss_g.at[c, k], rs_g.at[c, k], (me, sibling))

    def arrive(c):
        for k in range(NSEQ - 1):
            got_a(c, k).wait_recv()
        inbox[...] = rv_a[c]
        cols = pl.ds(pl.multiple_of(c * CC, 128), CC)
        for r in range(RCAP):
            one = pl.ds(clips[r], 1)
            rows = inbox[srcs[r]].astype(F32)
            shaped = rows * (1.0 + md[1, one, cols]) + md[0, one, cols]
            gath[c, group, r * BLOCK : (r + 1) * BLOCK, :] = shaped.astype(BF16)
        for k in (2, 1, 3):
            send_b(c, k).start()
        send_g(c, 0).start()

    def forward(c):
        for k in (1, 3, 2):
            got_b(c, k).wait_recv()
            send_g(c, k).start()

    def project(c):
        for k in range(Y):
            got_g(c, k).wait_recv()
        at = pl.ds(pl.multiple_of(c * CC, 128), CC)

        def tile(n, carry):
            left = gath[c].reshape(ALL, CC)
            acc[n] += jnp.dot(left, win[n, at, :], preferred_element_type=F32)
            return carry

        lax.fori_loop(0, 6, tile, 0)

    for i in (0, 3, 4, 5):
        loads[i].wait()

    def first_half(t, carry):
        @pl.when(t < NC)
        def _():
            arrive(t)

        @pl.when(jnp.logical_and(t >= 1, t < NC + 1))
        def _():
            forward(t - 1)

        @pl.when(t >= 2)
        def _():
            project(t - 2)

        return carry

    lax.fori_loop(0, NC + 2, first_half, 0)

    def rms(v):
        return v * lax.rsqrt(jnp.mean(v * v, axis=-1, keepdims=True) + EPSILON)

    def shape_rows(b, carry):
        at = pl.ds(pl.multiple_of(b * ROWS, BLOCK), ROWS)
        for i in range(2):
            part = slice(i * HD, (i + 1) * HD)
            qa[i, at, 0:HD] = rms(acc[0, at, part]).astype(BF16)
            ka[i, at, 0:HD] = rms(acc[1, at, part]).astype(BF16)
            va[i, at, 0:HD] = acc[2, at, part].astype(BF16)
        for n in range(3):
            v = acc[3 + n, at, :]
            inner = 0.7978845608 * (v + 0.044715 * (v * v * v))
            ah[at, ATT + n * TILE : ATT + (n + 1) * TILE] = (
                0.5 * v * (1.0 + jnp.tanh(inner))
            ).astype(BF16)
        return carry

    lax.fori_loop(0, NHEAD, shape_rows, 0)

    def attend(b, carry):
        at = pl.ds(pl.multiple_of(b * QT, QT), QT)
        for i in range(2):
            scores = lax.dot_general(
                qa[i, at, :], ka[i], (((1,), (1,)), ((), ())), preferred_element_type=F32
            )
            powers = jnp.exp2(scores * EXP_A - EXP_B).astype(BF16)
            mixed = jnp.dot(powers, va[i], preferred_element_type=F32)
            ah[at, i * HD : (i + 1) * HD] = (mixed[:, 0:HD] / mixed[:, HD:]).astype(BF16)
        return carry

    lax.fori_loop(0, ALL // QT, attend, 0)

    for i in (1, 2):
        loads[i].wait()

    def send_s(c):
        return remote(term.at[c, 1 - core], rv_s.at[c], ss_s.at[c], rs_s.at[c], (me, sibling))

    def part(c, dy, half):
        return term.at[c, core, (y + dy) % Y, pl.ds(half * HALF, HALF)]

    def send_f(c, i):
        return remote(
            part(c, 2, i), rv_f.at[c, i], ss_f.at[c, i], rs_f.at[c, i],
            (me, head_at(1 if i == 0 else 3)),
        )

    def send_n(c, i, half):
        dy = 1 if i == 0 else 3
        return remote(
            part(c, dy, half), rv_n.at[c, i, pl.ds(half * HALF, HALF)],
            ss_n.at[c, 2 * i + half], rs_n.at[c, 2 * i + half], (me, head_at(dy)),
        )

    def out_project(c):
        for side in range(2):
            p = 1 - core if side == 0 else core

            def tile(n, carry):
                at = pl.ds(pl.multiple_of(c * CC + n * TILE, TILE), TILE)
                left = ah[pl.ds(pl.multiple_of(p * (ALL // 2), BLOCK), ALL // 2), :]
                got = jnp.dot(left, wo[:, at], preferred_element_type=F32).astype(BF16)
                to = pl.ds(pl.multiple_of(n * TILE, TILE), TILE)
                term[c, p, :, :, to] = got.reshape(Y, ROWS, TILE)
                return carry

            lax.fori_loop(0, NT, tile, 0)
            if side == 0:
                send_s(c).start()

    def pair_sum(c):
        send_s(c).wait_recv()

        def add(i, carry):
            term[c, core, i] = (term[c, core, i].astype(F32) + rv_s[c, i].astype(F32)).astype(BF16)
            return carry

        lax.fori_loop(0, Y, add, 0)
        send_f(c, 0).start()
        send_f(c, 1).start()
        send_n(c, 0, 1).start()
        send_n(c, 1, 0).start()

    def relay(c):
        for i in range(2):
            send_f(c, i).wait_recv()
            ref = part(c, 1 if i == 0 else 3, i)
            ref[...] = (ref[...].astype(F32) + rv_f[c, i].astype(F32)).astype(BF16)
            send_n(c, i, i).start()

    def send_e(c, k):
        to = seq_at(*OFFSETS[k])
        return remote(st_e.at[c, to], rv_e.at[c, me], ss_e.at[c, k], rs_e.at[c, k], (to, head))

    def got_e(c, k):
        dz, dx = OFFSETS[k]
        frm = seq_at(Z - dz, X - dx)
        return remote(st_e.at[c, frm], rv_e.at[c, frm], ss_e.at[c, k], rs_e.at[c, k], (frm, head))

    def finish(c):
        for i in range(2):
            for half in range(2):
                send_n(c, i, half).wait_recv()
        cols = pl.ds(pl.multiple_of(c * CC, 128), CC)
        for r in range(RCAP):
            at = slice(r * BLOCK, (r + 1) * BLOCK)
            total = (
                term[c, core, y, at, :].astype(F32)
                + rv_n[c, 0, at, :].astype(F32)
                + rv_n[c, 1, at, :].astype(F32)
            )
            fin[c, r] = (total * md[2, pl.ds(clips[r], 1), cols]).astype(BF16)

        def stage_back(t, carry):
            st_e[c, t] = fin[c, ranks[t]]
            return carry

        lax.fori_loop(0, NSEQ, stage_back, 0)
        for k in range(NSEQ - 1):
            send_e(c, k).start()
        rv_e[c, me] = st_e[c, me]

    def second_half(t, carry):
        @pl.when(t < NC)
        def _():
            out_project(t)

        @pl.when(jnp.logical_and(t >= 1, t < NC + 1))
        def _():
            pair_sum(t - 1)

        @pl.when(jnp.logical_and(t >= 2, t < NC + 2))
        def _():
            relay(t - 2)

        @pl.when(t >= 3)
        def _():
            finish(t - 3)

        return carry

    lax.fori_loop(0, NC + 3, second_half, 0)

    def collect(c, carry):
        for k in range(NSEQ - 1):
            got_e(c, k).wait_recv()
        inbox[...] = rv_e[c]
        cols = pl.ds(pl.multiple_of(c * CC, 128), CC)
        for j in range(BLK_DEV):
            at = slice(j * BLOCK, (j + 1) * BLOCK)
            back = inbox[targets[j]].astype(F32)
            out[at, cols] = (tok[at, cols].astype(F32) + back).astype(BF16)
        return carry

    lax.fori_loop(0, NC, collect, 0)

    def drain(c, carry):
        for k in range(NSEQ - 1):
            send_a(c, k).wait_send()
            send_e(c, k).wait_send()
        for k in range(1, Y):
            send_b(c, k).wait_send()
        for k in range(Y):
            send_g(c, k).wait_send()
        send_s(c).wait_send()
        for i in range(2):
            send_f(c, i).wait_send()
            for half in range(2):
                send_n(c, i, half).wait_send()
        return carry

    lax.fori_loop(0, NC, drain, 0)


def body(
    tokens, block_target, clip_within, modulation,
    inner_attention, inner_hidden, outer_attention, outer_hidden,
):
    smem = pl.BlockSpec(memory_space=pltpu.SMEM)
    vmem = pl.BlockSpec(memory_space=pltpu.VMEM)
    anywhere = pl.BlockSpec(memory_space=pl.ANY)
    dma = pltpu.SemaphoreType.DMA
    return pl.pallas_call(
        kernel,
        out_shape=jax.ShapeDtypeStruct((BLK_DEV * BLOCK, D), BF16),
        in_specs=[smem, smem, vmem, vmem, anywhere, anywhere, anywhere, anywhere],
        out_specs=vmem,
        scratch_shapes=[
            pltpu.VMEM((BLK_DEV, BLOCK, D), BF16),
            pltpu.VMEM((NSEQ, BLOCK, CC), BF16),
            pltpu.VMEM((NC, NSEQ, BLOCK, CC), BF16),
            pltpu.VMEM((NC, NSEQ, BLOCK, CC), BF16),
            pltpu.VMEM((NC, NHEAD, ROWS, CC), BF16),
            pltpu.VMEM((6, D, TILE), BF16),
            pltpu.VMEM((ATT + HID, D), BF16),
            pltpu.VMEM((6, ALL, TILE), F32),
            pltpu.VMEM((2, ALL, 2 * HD), BF16),
            pltpu.VMEM((2, ALL, 2 * HD), BF16),
            pltpu.VMEM((2, ALL, 2 * HD), BF16),
            pltpu.VMEM((ALL, ATT + HID), BF16),
            pltpu.VMEM((NC, 2, Y, ROWS, CC), BF16),
            pltpu.VMEM((NC, Y, ROWS, CC), BF16),
            pltpu.VMEM((NC, 2, HALF, CC), BF16),
            pltpu.VMEM((NC, 2, ROWS, CC), BF16),
            pltpu.VMEM((NC, RCAP, BLOCK, CC), BF16),
            pltpu.VMEM((NC, NSEQ, BLOCK, CC), BF16),
            pltpu.VMEM((NC, NSEQ, BLOCK, CC), BF16),
            pltpu.SMEM((NSEQ,), jnp.int32),
            pltpu.SMEM((RCAP,), jnp.int32),
            pltpu.SMEM((RCAP,), jnp.int32),
            dma((6,)),
            dma((NC, NSEQ)), dma((NC, NSEQ)),
            dma((NC, Y)), dma((NC, Y)),
            dma((NC, Y)), dma((NC, Y)),
            dma((NC,)), dma((NC,)),
            dma((NC, 2)), dma((NC, 2)),
            dma((NC, 4)), dma((NC, 4)),
            dma((NC, NSEQ)), dma((NC, NSEQ)),
        ],
        compiler_params=pltpu.CompilerParams(
            collective_id=0, has_side_effects=True, vmem_limit_bytes=62 << 20
        ),
        cost_estimate=pl.CostEstimate(
            flops=13_000_000_000, bytes_accessed=17_000_000, transcendentals=2_000_000
        ),
    )(
        block_target, clip_within, tokens, jnp.transpose(modulation, (1, 0, 2)),
        jnp.transpose(inner_attention, (1, 0, 2)), inner_hidden, outer_attention, outer_hidden,
    )


def solution(mesh):
    placed = (
        P(("seq", "head"), None),
        P(),
        P(),
        P("seq", None, None),
        P(None, None, "head"),
        P(None, "head"),
        P("head", None),
        P("head", None),
    )
    return jax.shard_map(
        body, mesh=mesh, in_specs=placed, out_specs=P(("seq", "head"), None), check_vma=False
    )
```

```python
import math

import jax
import jax.numpy as jnp
from jax import lax
from jax.experimental import pallas as pl
from jax.experimental.pallas import tpu as pltpu
from jax.sharding import PartitionSpec as P

MESH = pl.DeviceIdType.MESH
F32 = jnp.float32
BF16 = jnp.bfloat16

HD = 128
BLOCK = 16
BLK_DEV = 4
CPG = 4
RCAP = 6
EPSILON = 1e-06

Z = 4
X = 4
NSEQ = Z * X
Y = 4
NHEAD = 8
D = 3072
ROWS = RCAP * BLOCK
ALL = NHEAD * ROWS
HALF = ROWS // 2
NC = 6
CC = D // NC
QT = 256
ATT = 256
HID = 768
PEERS = NSEQ - 1
AHEAD = 2
LAG_B = (1, 2, 3)
LAG_D = (1, 2, 3)
BIG = 1536.0
EXP_A = HD ** (-0.5) * math.log2(math.e)
EXP_B = BIG * EXP_A

OFFSETS = sorted(
    [(a, b) for a in range(Z) for b in range(X) if (a, b) != (0, 0)],
    key=lambda o: -(min(o[0], Z - o[0]) + min(o[1], X - o[1])),
)


def kernel(
    bt, cw, tok, md, wq, wh, woa, woh, out,
    nrm, inbox, st_a, rv_a, gath, win, wo, acc, qa, ka, va, ah,
    term, rv_s, rv_f, rv_n, fin, st_e, rv_e, ranks, srcs, clips,
    w_sem, ss_a, rs_a, ss_b, rs_b, rs_g,
    ss_d, rs_s, rs_f, rs_n, ss_e, rs_e,
):
    me = lax.axis_index("seq")
    head = lax.axis_index("head")
    z, x = me // X, me % X
    y, core = head // 2, head % 2
    sibling = head + 1 - 2 * core
    group = core * Y + y

    def seq_at(dz, dx):
        return ((z + dz) % Z) * X + (x + dx) % X

    def head_at(dy):
        return ((y + dy) % Y) * 2 + core

    def arrived(ref, sem):
        remote(ref, ref, sem, sem, (me, sibling)).wait_recv()

    def left(ref, sem):
        remote(ref, ref, sem, sem, (me, sibling)).wait_send()

    def remote(src, dst, ss, rs, dev):
        return pltpu.make_async_remote_copy(
            src_ref=src, dst_ref=dst, send_sem=ss, recv_sem=rs, device_id=dev, device_id_type=MESH
        )

    loads = [
        pltpu.make_async_copy(wq.at[n], win.at[0, :, pl.ds(n * ATT, ATT)], w_sem.at[n])
        for n in range(3)
    ] + [
        pltpu.make_async_copy(wh, win.at[1], w_sem.at[3]),
        pltpu.make_async_copy(woa, wo.at[pl.ds(0, ATT)], w_sem.at[4]),
        pltpu.make_async_copy(woh, wo.at[pl.ds(ATT, HID)], w_sem.at[5]),
    ]
    for load in loads:
        load.start()

    barrier = pltpu.get_barrier_semaphore()
    for dz, dx in OFFSETS:
        pl.semaphore_signal(barrier, inc=1, device_id=(seq_at(dz, dx), head), device_id_type=MESH)
    for dy in range(1, Y):
        pl.semaphore_signal(barrier, inc=1, device_id=(me, head_at(dy)), device_id_type=MESH)
    pl.semaphore_signal(barrier, inc=1, device_id=(me, sibling), device_id_type=MESH)

    for j in range(BLK_DEV):
        rows = tok[j * BLOCK : (j + 1) * BLOCK, :].astype(F32)
        centred = rows - jnp.mean(rows, axis=-1, keepdims=True)
        scale = lax.rsqrt(jnp.mean(centred * centred, axis=-1, keepdims=True) + EPSILON)
        nrm[j] = (centred * scale).astype(BF16)
    base = (me * NHEAD + head) * BLK_DEV
    targets = [bt[base + j] for j in range(BLK_DEV)]

    def stage(t, carry):
        pick = jnp.int32(0)
        for j in range(1, BLK_DEV):
            pick = jnp.where(targets[j] == t, j, pick)
        block = nrm[pick]
        for c in range(NC):
            st_a[c, t] = block[:, c * CC : (c + 1) * CC]
        return carry

    lax.fori_loop(0, NSEQ, stage, 0)
    pl.semaphore_wait(barrier, NSEQ - 1 + Y)

    def send_a(c, k):
        to = seq_at(*OFFSETS[k])
        return remote(st_a.at[c, to], rv_a.at[c, me], ss_a.at[c], rs_a.at[c], (to, head))

    def start_a(c):
        for k in range(PEERS):
            send_a(c, k).start()
        rv_a[c, me] = st_a[c, me]

    for c in range(AHEAD):
        start_a(c)

    def entry(s, h):
        live, clip = jnp.int32(0), jnp.int32(0)
        for j in range(BLK_DEV):
            at = (s * NHEAD + h) * BLK_DEV + j
            hit = bt[at] == me
            live = jnp.where(hit, 1, live)
            clip = jnp.where(hit, cw[at], clip)
        return live, clip

    def own_slot(s, carry):
        count, picked, named = carry
        live, clip = entry(s, head)
        ranks[s] = jnp.minimum(count, RCAP - 1)
        at = jnp.where(live == 1, count, -1)
        picked = tuple(jnp.where(at == r, s, picked[r]) for r in range(RCAP))
        named = tuple(jnp.where(at == r, clip, named[r]) for r in range(RCAP))
        return count + live, picked, named

    zeros = (jnp.int32(0),) * RCAP
    _, picked, named = lax.fori_loop(0, NSEQ, own_slot, (jnp.int32(0), zeros, zeros))
    for r in range(RCAP):
        srcs[r] = picked[r]
        clips[r] = named[r]

    lanes = lax.broadcasted_iota(jnp.int32, (BLOCK, HD), 1)

    def group_slots(g, carry):
        h = (g % Y) * 2 + g // Y

        def slot(s, carry):
            count, named = carry
            live, clip = entry(s, h)
            at = jnp.where(live == 1, count, -1)
            return count + live, tuple(jnp.where(at == r, clip, named[r]) for r in range(RCAP))

        dead = (jnp.int32(CPG),) * RCAP
        _, named = lax.fori_loop(0, NSEQ, slot, (jnp.int32(0), dead))
        for r in range(RCAP):
            one = jnp.where(lanes == named[r], 1.0, 0.0)
            at = pl.ds(pl.multiple_of(g * ROWS + r * BLOCK, BLOCK), BLOCK)
            for i in range(2):
                qa[i, at, HD:] = (one * BIG).astype(BF16)
                ka[i, at, HD:] = one.astype(BF16)
                va[i, at, HD:] = jnp.ones((BLOCK, HD), BF16)
        return carry

    lax.fori_loop(0, NHEAD, group_slots, 0)

    def clear(n, carry):
        acc[n] = jnp.zeros((ALL, HID), F32)
        return carry

    lax.fori_loop(0, 2, clear, 0)

    def own_rows(c):
        return gath.at[c, group]

    def rows_of(c, dy):
        return gath.at[c, core * Y + (y + dy) % Y]

    def send_b(c, k):
        return remote(own_rows(c), own_rows(c), ss_b.at[c], rs_b.at[c, k // 2], (me, head_at(k)))

    def pass_b(c, k):
        ref = rows_of(c, Y - k).at[pl.ds((k // 2) * HALF, HALF)]
        return remote(ref, ref, ss_b.at[c], rs_b.at[c, 2], (me, head_at(k)))

    def send_g(c, dy):
        ref = rows_of(c, dy)
        return remote(ref, ref, ss_b.at[c], rs_g.at[c], (me, sibling))

    def arrive(c):
        arrived(rv_a.at[c, pl.ds(0, PEERS)], rs_a.at[c])

        @pl.when(c + AHEAD < NC)
        def _():
            start_a(c + AHEAD)

        inbox[...] = rv_a[c]
        cols = pl.ds(pl.multiple_of(c * CC, 128), CC)
        for r in range(RCAP):
            one = pl.ds(clips[r], 1)
            rows = inbox[srcs[r]].astype(F32)
            shaped = rows * (1.0 + md[1, one, cols]) + md[0, one, cols]
            gath[c, group, r * BLOCK : (r + 1) * BLOCK, :] = shaped.astype(BF16)
        for k in (1, 3):
            send_b(c, k).start()
        send_g(c, 0).start()

    def forward_near(c):
        for k in (1, 3):
            arrived(rows_of(c, Y - k), rs_b.at[c, k // 2])
            pass_b(c, k).start()
            send_g(c, Y - k).start()

    def forward_far(c):
        arrived(rows_of(c, 2), rs_b.at[c, 2])
        send_g(c, 2).start()

    def project(c):
        arrived(gath.at[c, pl.ds((1 - core) * Y, Y)], rs_g.at[c])
        at = pl.ds(pl.multiple_of(c * CC, 128), CC)

        def tile(n, carry):
            rows = gath[c].reshape(ALL, CC)
            acc[n] += jnp.dot(rows, win[n, at, :], preferred_element_type=F32)
            return carry

        lax.fori_loop(0, 2, tile, 0)

    for i in range(4):
        loads[i].wait()

    def first_half(t, carry):
        @pl.when(t < NC)
        def _():
            arrive(t)

        for lag, step in zip(LAG_B, (forward_near, forward_far, project), strict=True):

            @pl.when(jnp.logical_and(t >= lag, t < NC + lag))
            def _(lag=lag, step=step):
                step(t - lag)

        return carry

    lax.fori_loop(0, NC + LAG_B[-1], first_half, 0)

    def rms(v):
        return v * lax.rsqrt(jnp.mean(v * v, axis=-1, keepdims=True) + EPSILON)

    def shape_rows(b, carry):
        at = pl.ds(pl.multiple_of(b * ROWS, BLOCK), ROWS)
        for i in range(2):
            part = [slice(n * ATT + i * HD, n * ATT + (i + 1) * HD) for n in range(3)]
            qa[i, at, 0:HD] = rms(acc[0, at, part[0]]).astype(BF16)
            ka[i, at, 0:HD] = rms(acc[0, at, part[1]]).astype(BF16)
            va[i, at, 0:HD] = acc[0, at, part[2]].astype(BF16)
        v = acc[1, at, :]
        inner = 0.7978845608 * (v + 0.044715 * (v * v * v))
        ah[at, ATT:] = (0.5 * v * (1.0 + jnp.tanh(inner))).astype(BF16)
        return carry

    lax.fori_loop(0, NHEAD, shape_rows, 0)

    def attend(b, carry):
        at = pl.ds(pl.multiple_of(b * QT, QT), QT)
        for i in range(2):
            scores = lax.dot_general(
                qa[i, at, :], ka[i], (((1,), (1,)), ((), ())), preferred_element_type=F32
            )
            powers = jnp.exp2(scores * EXP_A - EXP_B).astype(BF16)
            mixed = jnp.dot(powers, va[i], preferred_element_type=F32)
            ah[at, i * HD : (i + 1) * HD] = (mixed[:, 0:HD] / mixed[:, HD:]).astype(BF16)
        return carry

    lax.fori_loop(0, ALL // QT, attend, 0)

    for i in (4, 5):
        loads[i].wait()

    def send_s(c):
        return remote(term.at[c, 1 - core], rv_s.at[c], ss_d.at[c], rs_s.at[c], (me, sibling))

    def part(c, dy, half):
        return term.at[c, core, (y + dy) % Y, pl.ds(half * HALF, HALF)]

    def send_f(c, i):
        return remote(
            part(c, 2, i), rv_f.at[c, i], ss_d.at[c], rs_f.at[c, i],
            (me, head_at(1 if i == 0 else 3)),
        )

    def send_n(c, i, half):
        dy = 1 if i == 0 else 3
        return remote(
            part(c, dy, half), rv_n.at[c, i, pl.ds(half * HALF, HALF)],
            ss_d.at[c], rs_n.at[c], (me, head_at(dy)),
        )

    def out_project(c):
        for side in range(2):
            p = 1 - core if side == 0 else core

            at = pl.ds(pl.multiple_of(c * CC, 128), CC)
            rows = ah[pl.ds(pl.multiple_of(p * (ALL // 2), BLOCK), ALL // 2), :]
            got = jnp.dot(rows, wo[:, at], preferred_element_type=F32).astype(BF16)
            term[c, p] = got.reshape(Y, ROWS, CC)
            if side == 0:
                send_s(c).start()

    def pair_sum(c):
        send_s(c).wait_recv()

        def add(i, carry):
            term[c, core, i] = (term[c, core, i].astype(F32) + rv_s[c, i].astype(F32)).astype(BF16)
            return carry

        lax.fori_loop(0, Y, add, 0)
        send_f(c, 0).start()
        send_f(c, 1).start()
        send_n(c, 0, 1).start()
        send_n(c, 1, 0).start()

    def relay(c):
        for i in range(2):
            send_f(c, i).wait_recv()
            ref = part(c, 1 if i == 0 else 3, i)
            ref[...] = (ref[...].astype(F32) + rv_f[c, i].astype(F32)).astype(BF16)
            send_n(c, i, i).start()

    def send_e(c, k):
        to = seq_at(*OFFSETS[k])
        return remote(st_e.at[c, to], rv_e.at[c, me], ss_e.at[c], rs_e.at[c], (to, head))

    def finish(c):
        arrived(rv_n.at[c], rs_n.at[c])
        cols = pl.ds(pl.multiple_of(c * CC, 128), CC)
        for r in range(RCAP):
            at = slice(r * BLOCK, (r + 1) * BLOCK)
            total = (
                term[c, core, y, at, :].astype(F32)
                + rv_n[c, 0, at, :].astype(F32)
                + rv_n[c, 1, at, :].astype(F32)
            )
            fin[c, r] = (total * md[2, pl.ds(clips[r], 1), cols]).astype(BF16)

        def stage_back(t, carry):
            st_e[c, t] = fin[c, ranks[t]]
            return carry

        lax.fori_loop(0, NSEQ, stage_back, 0)
        for k in range(PEERS):
            send_e(c, k).start()
        rv_e[c, me] = st_e[c, me]

    def second_half(t, carry):
        @pl.when(t < NC)
        def _():
            out_project(t)

        for lag, step in zip(LAG_D, (pair_sum, relay, finish), strict=True):

            @pl.when(jnp.logical_and(t >= lag, t < NC + lag))
            def _(lag=lag, step=step):
                step(t - lag)

        return carry

    lax.fori_loop(0, NC + LAG_D[-1], second_half, 0)

    def collect(c, carry):
        arrived(rv_e.at[c, pl.ds(0, PEERS)], rs_e.at[c])
        inbox[...] = rv_e[c]
        cols = pl.ds(pl.multiple_of(c * CC, 128), CC)
        for j in range(BLK_DEV):
            at = slice(j * BLOCK, (j + 1) * BLOCK)
            back = inbox[targets[j]].astype(F32)
            out[at, cols] = (tok[at, cols].astype(F32) + back).astype(BF16)
        return carry

    lax.fori_loop(0, NC, collect, 0)

    def drain(c, carry):
        left(st_a.at[c, pl.ds(0, PEERS)], ss_a.at[c])
        left(st_e.at[c, pl.ds(0, PEERS)], ss_e.at[c])
        left(gath.at[c, pl.ds(0, 7)], ss_b.at[c])
        left(gath.at[c, pl.ds(0, 7)], ss_d.at[c])
        return carry

    lax.fori_loop(0, NC, drain, 0)


def body(
    tokens, block_target, clip_within, modulation,
    inner_attention, inner_hidden, outer_attention, outer_hidden,
):
    smem = pl.BlockSpec(memory_space=pltpu.SMEM)
    vmem = pl.BlockSpec(memory_space=pltpu.VMEM)
    anywhere = pl.BlockSpec(memory_space=pl.ANY)
    dma = pltpu.SemaphoreType.DMA
    return pl.pallas_call(
        kernel,
        out_shape=jax.ShapeDtypeStruct((BLK_DEV * BLOCK, D), BF16),
        in_specs=[smem, smem, vmem, vmem, anywhere, anywhere, anywhere, anywhere],
        out_specs=vmem,
        scratch_shapes=[
            pltpu.VMEM((BLK_DEV, BLOCK, D), BF16),
            pltpu.VMEM((NSEQ, BLOCK, CC), BF16),
            pltpu.VMEM((NC, NSEQ, BLOCK, CC), BF16),
            pltpu.VMEM((NC, NSEQ, BLOCK, CC), BF16),
            pltpu.VMEM((NC, NHEAD, ROWS, CC), BF16),
            pltpu.VMEM((2, D, HID), BF16),
            pltpu.VMEM((ATT + HID, D), BF16),
            pltpu.VMEM((2, ALL, HID), F32),
            pltpu.VMEM((2, ALL, 2 * HD), BF16),
            pltpu.VMEM((2, ALL, 2 * HD), BF16),
            pltpu.VMEM((2, ALL, 2 * HD), BF16),
            pltpu.VMEM((ALL, ATT + HID), BF16),
            pltpu.VMEM((NC, 2, Y, ROWS, CC), BF16),
            pltpu.VMEM((NC, Y, ROWS, CC), BF16),
            pltpu.VMEM((NC, 2, HALF, CC), BF16),
            pltpu.VMEM((NC, 2, ROWS, CC), BF16),
            pltpu.VMEM((NC, RCAP, BLOCK, CC), BF16),
            pltpu.VMEM((NC, NSEQ, BLOCK, CC), BF16),
            pltpu.VMEM((NC, NSEQ, BLOCK, CC), BF16),
            pltpu.SMEM((NSEQ,), jnp.int32),
            pltpu.SMEM((RCAP,), jnp.int32),
            pltpu.SMEM((RCAP,), jnp.int32),
            dma((6,)),
            dma((NC,)), dma((NC,)),
            dma((NC,)), dma((NC, Y - 1)), dma((NC,)),
            dma((NC,)), dma((NC,)), dma((NC, 2)), dma((NC,)),
            dma((NC,)), dma((NC,)),
        ],
        compiler_params=pltpu.CompilerParams(
            collective_id=0, has_side_effects=True, vmem_limit_bytes=62 << 20
        ),
        cost_estimate=pl.CostEstimate(
            flops=13_000_000_000, bytes_accessed=17_000_000, transcendentals=2_000_000
        ),
    )(
        block_target, clip_within, tokens, jnp.transpose(modulation, (1, 0, 2)),
        jnp.transpose(inner_attention, (1, 0, 2)), inner_hidden, outer_attention, outer_hidden,
    )


def solution(mesh):
    placed = (
        P(("seq", "head"), None),
        P(),
        P(),
        P("seq", None, None),
        P(None, None, "head"),
        P(None, "head"),
        P("head", None),
        P("head", None),
    )
    return jax.shard_map(
        body, mesh=mesh, in_specs=placed, out_specs=P(("seq", "head"), None), check_vma=False
    )
```

```python
import math

import jax
import jax.numpy as jnp
from jax import lax
from jax.experimental import pallas as pl
from jax.experimental.pallas import tpu as pltpu
from jax.sharding import PartitionSpec as P

MESH = pl.DeviceIdType.MESH
F32 = jnp.float32
BF16 = jnp.bfloat16

HD = 128
BLOCK = 16
BLK_DEV = 4
CPG = 4
RCAP = 6
EPSILON = 1e-06

Z = 4
X = 4
NSEQ = Z * X
Y = 4
NHEAD = 8
D = 3072
ROWS = RCAP * BLOCK
ALL = NHEAD * ROWS
HALF = ROWS // 2
NC = 6
CC = D // NC
ND = 6
CD = D // ND
QT = ALL // 2
ATT = 256
HID = 768
PEERS = NSEQ - 1
SLOT = {0: 0, 1: 1, 3: 2, 2: 3}
NEAR = 6
AHEAD = 3
LAG_B = (1, 3, 2)
LAG_D = (1, 2, 3)
BIG = 1536.0
EXP_A = HD ** (-0.5) * math.log2(math.e)
EXP_B = BIG * EXP_A

OFFSETS = sorted(
    [(a, b) for a in range(Z) for b in range(X) if (a, b) != (0, 0)],
    key=lambda o: -(min(o[0], Z - o[0]) + min(o[1], X - o[1])),
)


def kernel(
    bt, cw, tok, md, wq, wh, woa, woh, out,
    nrm, inbox, outbox, st_a, rv_a, gath, win, wo, acc, qa, ka, va, ah,
    term, rv_s, rv_f, rv_n, fin, st_e, rv_e, ranks, srcs, clips,
    w_sem, ss_a, rs_a, ss_b, rs_b, rs_g,
    ss_d, rs_s, rs_f, rs_n, ss_e, rs_e,
):
    me = lax.axis_index("seq")
    head = lax.axis_index("head")
    z, x = me // X, me % X
    y, core = head // 2, head % 2
    sibling = head + 1 - 2 * core

    def seq_at(dz, dx):
        return ((z + dz) % Z) * X + (x + dx) % X

    def head_at(dy):
        return ((y + dy) % Y) * 2 + core

    def arrived(ref, sem):
        remote(ref, ref, sem, sem, (me, sibling)).wait_recv()

    def left(ref, sem):
        remote(ref, ref, sem, sem, (me, sibling)).wait_send()

    def remote(src, dst, ss, rs, dev):
        return pltpu.make_async_remote_copy(
            src_ref=src, dst_ref=dst, send_sem=ss, recv_sem=rs, device_id=dev, device_id_type=MESH
        )

    loads = [
        pltpu.make_async_copy(wq.at[n], win.at[0, :, pl.ds(n * ATT, ATT)], w_sem.at[n])
        for n in range(3)
    ] + [
        pltpu.make_async_copy(wh, win.at[1], w_sem.at[3]),
        pltpu.make_async_copy(woa, wo.at[pl.ds(0, ATT)], w_sem.at[4]),
        pltpu.make_async_copy(woh, wo.at[pl.ds(ATT, HID)], w_sem.at[5]),
    ]
    for load in loads:
        load.start()

    barrier = pltpu.get_barrier_semaphore()
    for dz, dx in OFFSETS:
        pl.semaphore_signal(barrier, inc=1, device_id=(seq_at(dz, dx), head), device_id_type=MESH)
    for dy in range(1, Y):
        pl.semaphore_signal(barrier, inc=1, device_id=(me, head_at(dy)), device_id_type=MESH)
    pl.semaphore_signal(barrier, inc=1, device_id=(me, sibling), device_id_type=MESH)

    for j in range(BLK_DEV):
        rows = tok[j * BLOCK : (j + 1) * BLOCK, :].astype(F32)
        centred = rows - jnp.mean(rows, axis=-1, keepdims=True)
        scale = lax.rsqrt(jnp.mean(centred * centred, axis=-1, keepdims=True) + EPSILON)
        nrm[j] = (centred * scale).astype(BF16)
    base = (me * NHEAD + head) * BLK_DEV
    targets = [bt[base + j] for j in range(BLK_DEV)]

    def stage(t, carry):
        pick = jnp.int32(0)
        for j in range(1, BLK_DEV):
            pick = jnp.where(targets[j] == t, j, pick)
        block = nrm[pick]
        for c in range(NC):
            st_a[c, t] = block[:, c * CC : (c + 1) * CC]
        return carry

    lax.fori_loop(0, NSEQ, stage, 0)
    pl.semaphore_wait(barrier, NSEQ - 1 + Y)

    def send_a(c, k):
        to = seq_at(*OFFSETS[k])
        return remote(st_a.at[c, to], rv_a.at[c, me], ss_a.at[c], rs_a.at[c], (to, head))

    def start_a(c):
        for k in range(PEERS):
            send_a(c, k).start()
        rv_a[c, me] = st_a[c, me]

    for c in range(AHEAD):
        start_a(c)

    def entry(s, h):
        live, clip = jnp.int32(0), jnp.int32(0)
        for j in range(BLK_DEV):
            at = (s * NHEAD + h) * BLK_DEV + j
            hit = bt[at] == me
            live = jnp.where(hit, 1, live)
            clip = jnp.where(hit, cw[at], clip)
        return live, clip

    def own_slot(s, carry):
        count, picked, named = carry
        live, clip = entry(s, head)
        ranks[s] = jnp.minimum(count, RCAP - 1)
        at = jnp.where(live == 1, count, -1)
        picked = tuple(jnp.where(at == r, s, picked[r]) for r in range(RCAP))
        named = tuple(jnp.where(at == r, clip, named[r]) for r in range(RCAP))
        return count + live, picked, named

    zeros = (jnp.int32(0),) * RCAP
    _, picked, named = lax.fori_loop(0, NSEQ, own_slot, (jnp.int32(0), zeros, zeros))
    for r in range(RCAP):
        srcs[r] = picked[r]
        clips[r] = named[r]

    lanes = lax.broadcasted_iota(jnp.int32, (BLOCK, HD), 1)

    def group_slots(g, carry):
        place = g // 2
        dy = place + place // 2 - 2 * (place // 3)
        h = ((y + dy) % Y) * 2 + g % 2

        def slot(s, carry):
            count, named = carry
            live, clip = entry(s, h)
            at = jnp.where(live == 1, count, -1)
            return count + live, tuple(jnp.where(at == r, clip, named[r]) for r in range(RCAP))

        dead = (jnp.int32(CPG),) * RCAP
        _, named = lax.fori_loop(0, NSEQ, slot, (jnp.int32(0), dead))
        for r in range(RCAP):
            one = jnp.where(lanes == named[r], 1.0, 0.0)
            at = pl.ds(pl.multiple_of(g * ROWS + r * BLOCK, BLOCK), BLOCK)
            for i in range(2):
                qa[i, at, HD:] = (one * BIG).astype(BF16)
                ka[i, at, HD:] = one.astype(BF16)
                va[i, at, HD:] = jnp.ones((BLOCK, HD), BF16)
        return carry

    def clear(n, carry):
        acc[n] = jnp.zeros((ALL, HID), F32)
        return carry

    lax.fori_loop(0, 2, clear, 0)

    def send_b(c, k):
        return remote(
            gath.at[c, 0, core], gath.at[c, SLOT[Y - k], core],
            ss_b.at[c, 0], rs_b.at[c, k // 2], (me, head_at(k)),
        )

    def pass_b(c, k):
        half = pl.ds((k // 2) * HALF, HALF)
        return remote(
            gath.at[c, SLOT[Y - k], core, half], gath.at[c, SLOT[2], core, half],
            ss_b.at[c, 0], rs_b.at[c, 2], (me, head_at(k)),
        )

    def send_g(c, slot):
        ref = gath.at[c, slot, core]
        return remote(ref, ref, ss_b.at[c, 1], rs_g.at[c, slot // 3], (me, sibling))

    def arrive(c):
        arrived(rv_a.at[c, pl.ds(0, PEERS)], rs_a.at[c])

        @pl.when(c + AHEAD < NC)
        def _():
            start_a(c + AHEAD)

        inbox[...] = rv_a[c]
        cols = pl.ds(pl.multiple_of(c * CC, 128), CC)
        for r in range(RCAP):
            one = pl.ds(clips[r], 1)
            rows = inbox[srcs[r]].astype(F32)
            shaped = rows * (1.0 + md[1, one, cols]) + md[0, one, cols]
            gath[c, 0, core, r * BLOCK : (r + 1) * BLOCK, :] = shaped.astype(BF16)
        for k in (1, 3):
            send_b(c, k).start()
        send_g(c, 0).start()

    def forward_near(c):
        for k in (1, 3):
            slot = SLOT[Y - k]
            arrived(gath.at[c, slot, core], rs_b.at[c, k // 2])
            pass_b(c, k).start()
            send_g(c, slot).start()

    def forward_far(c):
        arrived(gath.at[c, 3, core], rs_b.at[c, 2])
        send_g(c, 3).start()

    def project_rows(c, slots):
        rows = len(slots) * 2 * ROWS
        at = pl.ds(pl.multiple_of(c * CC, 128), CC)
        to = pl.ds(slots[0] * 2 * ROWS, rows)

        def tile(n, carry):
            left = gath[c, slots[0] : slots[-1] + 1].reshape(rows, CC)
            acc[n, to, :] += jnp.dot(left, win[n, at, :], preferred_element_type=F32)
            return carry

        lax.fori_loop(0, 2, tile, 0)

    def rms(v):
        return v * lax.rsqrt(jnp.mean(v * v, axis=-1, keepdims=True) + EPSILON)

    def shape_rows(b, carry):
        at = pl.ds(pl.multiple_of(b * ROWS, BLOCK), ROWS)
        for i in range(2):
            part = [slice(n * ATT + i * HD, n * ATT + (i + 1) * HD) for n in range(3)]
            qa[i, at, 0:HD] = rms(acc[0, at, part[0]]).astype(BF16)
            ka[i, at, 0:HD] = rms(acc[0, at, part[1]]).astype(BF16)
            va[i, at, 0:HD] = acc[0, at, part[2]].astype(BF16)
        v = acc[1, at, :]
        inner = 0.7978845608 * (v + 0.044715 * (v * v * v))
        ah[b // 2, b % 2, :, ATT:] = (0.5 * v * (1.0 + jnp.tanh(inner))).astype(BF16)
        return carry

    def project(c):
        near = gath.at[c, pl.ds(0, 3), 1 - core]
        far = gath.at[c, 3, 1 - core]

        @pl.when(c < NC - 1)
        def _():
            arrived(near, rs_g.at[c, 0])
            arrived(far, rs_g.at[c, 1])
            project_rows(c, range(Y))

        @pl.when(c == NC - 1)
        def _():
            arrived(near, rs_g.at[c, 0])
            project_rows(c, range(3))
            lax.fori_loop(0, NEAR, shape_rows, 0)
            arrived(far, rs_g.at[c, 1])
            project_rows(c, range(3, Y))
            lax.fori_loop(NEAR, NHEAD, shape_rows, 0)

    for i in range(4):
        loads[i].wait()

    def first_half(t, carry):
        @pl.when(t < NC)
        def _():
            arrive(t)

        @pl.when(t < NHEAD)
        def _():
            group_slots(t, 0)

        for lag, step in zip(LAG_B, (forward_near, project, forward_far), strict=True):

            @pl.when(jnp.logical_and(t >= lag, t < NC + lag))
            def _(lag=lag, step=step):
                step(t - lag)

        return carry

    lax.fori_loop(0, NC + max(LAG_B), first_half, 0)

    def attend(b, carry):
        at = pl.ds(pl.multiple_of(b * QT, QT), QT)
        for i in range(2):
            scores = lax.dot_general(
                qa[i, at, :], ka[i], (((1,), (1,)), ((), ())), preferred_element_type=F32
            )
            powers = jnp.exp2(scores * EXP_A - EXP_B).astype(BF16)
            mixed = jnp.dot(powers, va[i], preferred_element_type=F32)
            found = (mixed[:, 0:HD] / mixed[:, HD:]).astype(BF16)
            ah[pl.ds(b * 2, 2), :, :, i * HD : (i + 1) * HD] = found.reshape(2, 2, ROWS, HD)
        return carry

    lax.fori_loop(0, ALL // QT, attend, 0)

    for i in (4, 5):
        loads[i].wait()

    def send_s(c):
        return remote(term.at[c, :, 1 - core], rv_s.at[c], ss_d.at[c, 1], rs_s.at[c], (me, sibling))

    def part(c, slot, half):
        return term.at[c, slot, core, pl.ds(half * HALF, HALF)]

    def send_f(c, i):
        return remote(
            part(c, 3, i), rv_f.at[c, i], ss_d.at[c, 0], rs_f.at[c, i],
            (me, head_at(1 if i == 0 else 3)),
        )

    def send_n(c, i, half):
        dy = 1 if i == 0 else 3
        return remote(
            part(c, 1 + i, half), rv_n.at[c, i, pl.ds(half * HALF, HALF)],
            ss_d.at[c, 0], rs_n.at[c], (me, head_at(dy)),
        )

    def out_project(c):
        for side in range(2):
            p = 1 - core if side == 0 else core

            at = pl.ds(pl.multiple_of(c * CD, 128), CD)
            rows = ah[:, p].reshape(ALL // 2, ATT + HID)
            got = jnp.dot(rows, wo[:, at], preferred_element_type=F32).astype(BF16)
            term[c, :, p] = got.reshape(Y, ROWS, CD)
            if side == 0:
                send_s(c).start()

    def pair_sum(c):
        send_s(c).wait_recv()

        def add(i):
            term[c, i, core] = (term[c, i, core].astype(F32) + rv_s[c, i].astype(F32)).astype(BF16)

        add(3)
        send_f(c, 0).start()
        send_f(c, 1).start()
        add(1)
        send_n(c, 0, 1).start()
        add(2)
        send_n(c, 1, 0).start()
        add(0)

    def relay(c):
        for i in range(2):
            send_f(c, i).wait_recv()
            ref = part(c, 1 + i, i)
            ref[...] = (ref[...].astype(F32) + rv_f[c, i].astype(F32)).astype(BF16)
            send_n(c, i, i).start()

    def send_e(c, k):
        to = seq_at(*OFFSETS[k])
        return remote(st_e.at[c, to], rv_e.at[c, me], ss_e.at[c], rs_e.at[c], (to, head))

    def finish(c):
        arrived(rv_n.at[c], rs_n.at[c])
        cols = pl.ds(pl.multiple_of(c * CD, 128), CD)
        for r in range(RCAP):
            at = slice(r * BLOCK, (r + 1) * BLOCK)
            total = (
                term[c, 0, core, at, :].astype(F32)
                + rv_n[c, 0, at, :].astype(F32)
                + rv_n[c, 1, at, :].astype(F32)
            )
            fin[c, r] = (total * md[2, pl.ds(clips[r], 1), cols]).astype(BF16)

        def stage_back(t, carry):
            st_e[c, t] = fin[c, ranks[t]]
            return carry

        lax.fori_loop(0, NSEQ, stage_back, 0)
        for k in range(PEERS):
            send_e(c, k).start()
        rv_e[c, me] = st_e[c, me]

    def second_half(t, carry):
        @pl.when(t < ND)
        def _():
            out_project(t)

        for lag, step in zip(LAG_D, (pair_sum, relay, finish), strict=True):

            @pl.when(jnp.logical_and(t >= lag, t < ND + lag))
            def _(lag=lag, step=step):
                step(t - lag)

        return carry

    lax.fori_loop(0, ND + LAG_D[-1], second_half, 0)

    def collect(c, carry):
        arrived(rv_e.at[c, pl.ds(0, PEERS)], rs_e.at[c])
        outbox[...] = rv_e[c]
        cols = pl.ds(pl.multiple_of(c * CD, 128), CD)
        for j in range(BLK_DEV):
            at = slice(j * BLOCK, (j + 1) * BLOCK)
            back = outbox[targets[j]].astype(F32)
            out[at, cols] = (tok[at, cols].astype(F32) + back).astype(BF16)
        return carry

    lax.fori_loop(0, ND, collect, 0)

    def drain_a(c, carry):
        left(st_a.at[c, pl.ds(0, PEERS)], ss_a.at[c])
        left(gath.at[c, pl.ds(0, 3), 0], ss_b.at[c, 0])
        left(gath.at[c, :, 0], ss_b.at[c, 1])
        return carry

    lax.fori_loop(0, NC, drain_a, 0)

    def drain_d(c, carry):
        left(st_e.at[c, pl.ds(0, PEERS)], ss_e.at[c])
        left(term.at[c, pl.ds(0, 3), 0], ss_d.at[c, 0])
        left(term.at[c, :, 0], ss_d.at[c, 1])
        return carry

    lax.fori_loop(0, ND, drain_d, 0)


def body(
    tokens, block_target, clip_within, modulation,
    inner_attention, inner_hidden, outer_attention, outer_hidden,
):
    smem = pl.BlockSpec(memory_space=pltpu.SMEM)
    vmem = pl.BlockSpec(memory_space=pltpu.VMEM)
    anywhere = pl.BlockSpec(memory_space=pl.ANY)
    dma = pltpu.SemaphoreType.DMA
    return pl.pallas_call(
        kernel,
        out_shape=jax.ShapeDtypeStruct((BLK_DEV * BLOCK, D), BF16),
        in_specs=[smem, smem, vmem, vmem, anywhere, anywhere, anywhere, anywhere],
        out_specs=vmem,
        scratch_shapes=[
            pltpu.VMEM((BLK_DEV, BLOCK, D), BF16),
            pltpu.VMEM((NSEQ, BLOCK, CC), BF16),
            pltpu.VMEM((NSEQ, BLOCK, CD), BF16),
            pltpu.VMEM((NC, NSEQ, BLOCK, CC), BF16),
            pltpu.VMEM((NC, NSEQ, BLOCK, CC), BF16),
            pltpu.VMEM((NC, Y, 2, ROWS, CC), BF16),
            pltpu.VMEM((2, D, HID), BF16),
            pltpu.VMEM((ATT + HID, D), BF16),
            pltpu.VMEM((2, ALL, HID), F32),
            pltpu.VMEM((2, ALL, 2 * HD), BF16),
            pltpu.VMEM((2, ALL, 2 * HD), BF16),
            pltpu.VMEM((2, ALL, 2 * HD), BF16),
            pltpu.VMEM((Y, 2, ROWS, ATT + HID), BF16),
            pltpu.VMEM((ND, Y, 2, ROWS, CD), BF16),
            pltpu.VMEM((ND, Y, ROWS, CD), BF16),
            pltpu.VMEM((ND, 2, HALF, CD), BF16),
            pltpu.VMEM((ND, 2, ROWS, CD), BF16),
            pltpu.VMEM((ND, RCAP, BLOCK, CD), BF16),
            pltpu.VMEM((ND, NSEQ, BLOCK, CD), BF16),
            pltpu.VMEM((ND, NSEQ, BLOCK, CD), BF16),
            pltpu.SMEM((NSEQ,), jnp.int32),
            pltpu.SMEM((RCAP,), jnp.int32),
            pltpu.SMEM((RCAP,), jnp.int32),
            dma((6,)),
            dma((NC,)), dma((NC,)),
            dma((NC, 2)), dma((NC, Y - 1)), dma((NC, 2)),
            dma((ND, 2)), dma((ND,)), dma((ND, 2)), dma((ND,)),
            dma((ND,)), dma((ND,)),
        ],
        compiler_params=pltpu.CompilerParams(
            collective_id=0, has_side_effects=True, vmem_limit_bytes=62 << 20
        ),
        cost_estimate=pl.CostEstimate(
            flops=13_000_000_000, bytes_accessed=17_000_000, transcendentals=2_000_000
        ),
    )(
        block_target, clip_within, tokens, jnp.transpose(modulation, (1, 0, 2)),
        jnp.transpose(inner_attention, (1, 0, 2)), inner_hidden, outer_attention, outer_hidden,
    )


def solution(mesh):
    placed = (
        P(("seq", "head"), None),
        P(),
        P(),
        P("seq", None, None),
        P(None, None, "head"),
        P(None, "head"),
        P("head", None),
        P("head", None),
    )
    return jax.shard_map(
        body, mesh=mesh, in_specs=placed, out_specs=P(("seq", "head"), None), check_vma=False
    )
```

```python
import math

import jax
import jax.numpy as jnp
from jax import lax
from jax.experimental import pallas as pl
from jax.experimental.pallas import tpu as pltpu
from jax.sharding import PartitionSpec as P

MESH = pl.DeviceIdType.MESH
F32 = jnp.float32
BF16 = jnp.bfloat16

HD = 128
BLOCK = 16
BLK_DEV = 4
CPG = 4
RCAP = 6
EPSILON = 1e-06

Z = 4
X = 4
NSEQ = Z * X
Y = 4
NHEAD = 8
D = 3072
ROWS = RCAP * BLOCK
ALL = NHEAD * ROWS
HALF = ROWS // 2
FIRST = (2, 4, 4, 4, 4, 4, 2)
SECOND = (4, 4, 4, 4, 4, 4)
NC = len(FIRST)
ND = len(SECOND)
QT = ALL // 2
ATT = 256
HID = 768
PEERS = NSEQ - 1
SLOT = {0: 0, 1: 1, 3: 2, 2: 3}
NEAR = 6
AHEAD = 3
LAG_B = (1, 3, 2)
LAG_D = (1, 2, 3)
BIG = 256.0
EXP_A = HD ** (-0.5) * math.log2(math.e)


def spans(widths):
    starts = [128 * sum(widths[:i]) for i in range(len(widths))]
    return [slice(a, a + 128 * w) for a, w in zip(starts, widths, strict=True)]


COLS = spans(FIRST)
BACK = spans(SECOND)

OFFSETS = sorted(
    [(a, b) for a in range(Z) for b in range(X) if (a, b) != (0, 0)],
    key=lambda o: -(min(o[0], Z - o[0]) + min(o[1], X - o[1])),
)


def kernel(
    bt, cw, tok, md, wq, wh, woa, woh, out,
    nrm, inbox, outbox, st_a, rv_a, gath, win, wo, acc, qa, ka, va, ah,
    term, rv_s, rv_f, rv_n, fin, st_e, rv_e, ranks, srcs, clips,
    w_sem, ss_a, rs_a, ss_b, rs_b, rs_g,
    ss_d, rs_s, rs_f, rs_n, ss_e, rs_e,
):
    me = lax.axis_index("seq")
    head = lax.axis_index("head")
    z, x = me // X, me % X
    y, core = head // 2, head % 2
    sibling = head + 1 - 2 * core

    def seq_at(dz, dx):
        return ((z + dz) % Z) * X + (x + dx) % X

    def head_at(dy):
        return ((y + dy) % Y) * 2 + core

    def arrived(ref, sem):
        remote(ref, ref, sem, sem, (me, sibling)).wait_recv()

    def left(ref, sem):
        remote(ref, ref, sem, sem, (me, sibling)).wait_send()

    def remote(src, dst, ss, rs, dev):
        return pltpu.make_async_remote_copy(
            src_ref=src, dst_ref=dst, send_sem=ss, recv_sem=rs, device_id=dev, device_id_type=MESH
        )

    loads = [
        pltpu.make_async_copy(wq.at[n], win.at[0, :, pl.ds(n * ATT, ATT)], w_sem.at[n])
        for n in range(3)
    ] + [
        pltpu.make_async_copy(wh, win.at[1], w_sem.at[3]),
        pltpu.make_async_copy(woa, wo.at[pl.ds(0, ATT)], w_sem.at[4]),
        pltpu.make_async_copy(woh, wo.at[pl.ds(ATT, HID)], w_sem.at[5]),
    ]
    for load in loads:
        load.start()

    barrier = pltpu.get_barrier_semaphore()
    for dz, dx in OFFSETS:
        pl.semaphore_signal(barrier, inc=1, device_id=(seq_at(dz, dx), head), device_id_type=MESH)
    for dy in range(1, Y):
        pl.semaphore_signal(barrier, inc=1, device_id=(me, head_at(dy)), device_id_type=MESH)
    pl.semaphore_signal(barrier, inc=1, device_id=(me, sibling), device_id_type=MESH)

    for j in range(BLK_DEV):
        rows = tok[j * BLOCK : (j + 1) * BLOCK, :].astype(F32)
        centred = rows - jnp.mean(rows, axis=-1, keepdims=True)
        scale = lax.rsqrt(jnp.mean(centred * centred, axis=-1, keepdims=True) + EPSILON)
        nrm[j] = (centred * scale).astype(BF16)
    base = (me * NHEAD + head) * BLK_DEV
    targets = [bt[base + j] for j in range(BLK_DEV)]

    def stage(t, carry):
        pick = jnp.int32(0)
        for j in range(1, BLK_DEV):
            pick = jnp.where(targets[j] == t, j, pick)
        st_a[t] = nrm[pick]
        return carry

    lax.fori_loop(0, NSEQ, stage, 0)
    pl.semaphore_wait(barrier, NSEQ - 1 + Y)

    def send_a(c, k):
        to = seq_at(*OFFSETS[k])
        return remote(st_a.at[to, :, COLS[c]], rv_a.at[me, :, COLS[c]], ss_a.at[c], rs_a.at[c], (to, head))

    def start_a(c):
        for k in range(PEERS):
            send_a(c, k).start()
        rv_a[me, :, COLS[c]] = st_a[me, :, COLS[c]]

    start_a(0)

    def entry(s, h):
        live, clip = jnp.int32(0), jnp.int32(0)
        for j in range(BLK_DEV):
            at = (s * NHEAD + h) * BLK_DEV + j
            hit = bt[at] == me
            live = jnp.where(hit, 1, live)
            clip = jnp.where(hit, cw[at], clip)
        return live, clip

    def own_slot(s, carry):
        count, picked, named = carry
        live, clip = entry(s, head)
        ranks[s] = jnp.minimum(count, RCAP - 1)
        at = jnp.where(live == 1, count, -1)
        picked = tuple(jnp.where(at == r, s, picked[r]) for r in range(RCAP))
        named = tuple(jnp.where(at == r, clip, named[r]) for r in range(RCAP))
        return count + live, picked, named

    zeros = (jnp.int32(0),) * RCAP
    _, picked, named = lax.fori_loop(0, NSEQ, own_slot, (jnp.int32(0), zeros, zeros))
    for r in range(RCAP):
        srcs[r] = picked[r]
        clips[r] = named[r]

    lanes = lax.broadcasted_iota(jnp.int32, (BLOCK, HD), 1)

    def group_slots(g, carry):
        place = g // 2
        dy = place + place // 2 - 2 * (place // 3)
        h = ((y + dy) % Y) * 2 + g % 2

        def slot(s, carry):
            count, named = carry
            live, clip = entry(s, h)
            at = jnp.where(live == 1, count, -1)
            return count + live, tuple(jnp.where(at == r, clip, named[r]) for r in range(RCAP))

        dead = (jnp.int32(CPG),) * RCAP
        _, named = lax.fori_loop(0, NSEQ, slot, (jnp.int32(0), dead))
        for r in range(RCAP):
            same = jnp.where(lanes == named[r], 1.0, 0.0)
            always = jnp.where(lanes == CPG + 1, 1.0, 0.0)
            at = pl.ds(pl.multiple_of(g * ROWS + r * BLOCK, BLOCK), BLOCK)
            for i in range(2):
                qa[i, at, HD:] = ((same - always) * BIG).astype(BF16)
                ka[i, at, HD:] = (same + always).astype(BF16)
                va[i, at, HD:] = jnp.ones((BLOCK, HD), BF16)
        return carry

    def clear(n, carry):
        acc[n] = jnp.zeros((ALL, HID), F32)
        return carry

    lax.fori_loop(0, 2, clear, 0)

    for c in range(1, AHEAD):
        start_a(c)

    def send_b(c, k):
        return remote(
            gath.at[0, core, :, COLS[c]], gath.at[SLOT[Y - k], core, :, COLS[c]],
            ss_b.at[c, 0], rs_b.at[c, k // 2], (me, head_at(k)),
        )

    def pass_b(c, k):
        half = pl.ds((k // 2) * HALF, HALF)
        return remote(
            gath.at[SLOT[Y - k], core, half, COLS[c]], gath.at[SLOT[2], core, half, COLS[c]],
            ss_b.at[c, 0], rs_b.at[c, 2], (me, head_at(k)),
        )

    def send_g(c, slot):
        ref = gath.at[slot, core, :, COLS[c]]
        return remote(ref, ref, ss_b.at[c, 1], rs_g.at[c, slot // 3], (me, sibling))

    def arrive(c):
        cols = COLS[c]
        wide = slice(0, cols.stop - cols.start)
        arrived(rv_a.at[0:PEERS, :, cols], rs_a.at[c])
        if c + AHEAD < NC:
            start_a(c + AHEAD)
        inbox[:, :, wide] = rv_a[:, :, cols]
        for r in range(RCAP):
            one = pl.ds(clips[r], 1)
            rows = inbox[srcs[r], :, wide].astype(F32)
            shaped = rows * (1.0 + md[1, one, cols]) + md[0, one, cols]
            gath[0, core, r * BLOCK : (r + 1) * BLOCK, cols] = shaped.astype(BF16)
        for k in (1, 3):
            send_b(c, k).start()
        send_g(c, 0).start()

    def forward_near(c):
        for k in (1, 3):
            slot = SLOT[Y - k]
            arrived(gath.at[slot, core, :, COLS[c]], rs_b.at[c, k // 2])
            pass_b(c, k).start()
            send_g(c, slot).start()

    def forward_far(c):
        arrived(gath.at[3, core, :, COLS[c]], rs_b.at[c, 2])
        send_g(c, 3).start()

    def project_rows(c, slots):
        rows = len(slots) * 2 * ROWS
        cols = COLS[c]
        to = pl.ds(slots[0] * 2 * ROWS, rows)

        def tile(n, carry):
            lhs = gath[slots[0] : slots[-1] + 1, :, :, cols].reshape(rows, cols.stop - cols.start)
            acc[n, to, :] += jnp.dot(lhs, win[n, cols, :], preferred_element_type=F32)
            return carry

        lax.fori_loop(0, 2, tile, 0)

    def rms(v):
        return v * lax.rsqrt(jnp.mean(v * v, axis=-1, keepdims=True) + EPSILON)

    def shape_rows(b, carry):
        at = pl.ds(pl.multiple_of(b * ROWS, BLOCK), ROWS)
        for i in range(2):
            part = [slice(n * ATT + i * HD, n * ATT + (i + 1) * HD) for n in range(3)]
            qa[i, at, 0:HD] = (rms(acc[0, at, part[0]]) * EXP_A).astype(BF16)
            ka[i, at, 0:HD] = rms(acc[0, at, part[1]]).astype(BF16)
            va[i, at, 0:HD] = acc[0, at, part[2]].astype(BF16)
        v = acc[1, at, :]
        inner = 0.7978845608 * (v + 0.044715 * (v * v * v))
        ah[b // 2, b % 2, :, ATT:] = (0.5 * v * (1.0 + jnp.tanh(inner))).astype(BF16)
        return carry

    def project(c):
        near = gath.at[0:3, 1 - core, :, COLS[c]]
        far = gath.at[3, 1 - core, :, COLS[c]]
        arrived(near, rs_g.at[c, 0])
        if c < NC - 1:
            arrived(far, rs_g.at[c, 1])
            project_rows(c, range(Y))
            return
        project_rows(c, range(3))
        lax.fori_loop(0, NEAR, shape_rows, 0)
        arrived(far, rs_g.at[c, 1])
        project_rows(c, range(3, Y))
        lax.fori_loop(NEAR, NHEAD, shape_rows, 0)

    for i in range(4):
        loads[i].wait()

    for t in range(NC + max(LAG_B)):
        if t < NC:
            arrive(t)
        if t < NHEAD:
            group_slots(t, 0)
        for lag, step in zip(LAG_B, (forward_near, project, forward_far), strict=True):
            if lag <= t < NC + lag:
                step(t - lag)

    def attend(b, carry):
        at = pl.ds(pl.multiple_of(b * QT, QT), QT)
        for i in range(2):
            scores = lax.dot_general(
                qa[i, at, :], ka[i], (((1,), (1,)), ((), ())), preferred_element_type=F32
            )
            powers = jnp.exp2(scores).astype(BF16)
            mixed = jnp.dot(powers, va[i], preferred_element_type=F32)
            found = (mixed[:, 0:HD] / mixed[:, HD:]).astype(BF16)
            ah[pl.ds(b * 2, 2), :, :, i * HD : (i + 1) * HD] = found.reshape(2, 2, ROWS, HD)
        return carry

    lax.fori_loop(0, ALL // QT, attend, 0)

    for i in (4, 5):
        loads[i].wait()

    def send_s(c):
        ref = term.at[:, 1 - core, :, BACK[c]]
        return remote(ref, rv_s.at[:, :, BACK[c]], ss_d.at[c, 1], rs_s.at[c], (me, sibling))

    def part(c, slot, half):
        return term.at[slot, core, pl.ds(half * HALF, HALF), BACK[c]]

    def send_f(c, i):
        return remote(
            part(c, 3, i), rv_f.at[i, :, BACK[c]], ss_d.at[c, 0], rs_f.at[c, i],
            (me, head_at(1 if i == 0 else 3)),
        )

    def send_n(c, i, half):
        dy = 1 if i == 0 else 3
        return remote(
            part(c, 1 + i, half), rv_n.at[i, pl.ds(half * HALF, HALF), BACK[c]],
            ss_d.at[c, 0], rs_n.at[c], (me, head_at(dy)),
        )

    def out_project(c):
        for side in range(2):
            p = 1 - core if side == 0 else core

            cols = BACK[c]
            rows = ah[:, p].reshape(ALL // 2, ATT + HID)
            got = jnp.dot(rows, wo[:, cols], preferred_element_type=F32).astype(BF16)
            term[:, p, :, cols] = got.reshape(Y, ROWS, cols.stop - cols.start)
            if side == 0:
                send_s(c).start()

    def pair_sum(c):
        send_s(c).wait_recv()

        def add(i):
            both = term[i, core, :, BACK[c]].astype(F32) + rv_s[i, :, BACK[c]].astype(F32)
            term[i, core, :, BACK[c]] = both.astype(BF16)

        add(3)
        send_f(c, 0).start()
        send_f(c, 1).start()
        add(1)
        send_n(c, 0, 1).start()
        add(2)
        send_n(c, 1, 0).start()
        add(0)

    def relay(c):
        for i in range(2):
            send_f(c, i).wait_recv()
            ref = part(c, 1 + i, i)
            ref[...] = (ref[...].astype(F32) + rv_f[i, :, BACK[c]].astype(F32)).astype(BF16)
            send_n(c, i, i).start()

    def send_e(c, k):
        to = seq_at(*OFFSETS[k])
        return remote(st_e.at[to, :, BACK[c]], rv_e.at[me, :, BACK[c]], ss_e.at[c], rs_e.at[c], (to, head))

    def finish(c):
        cols = BACK[c]
        arrived(rv_n.at[:, :, cols], rs_n.at[c])
        for r in range(RCAP):
            at = slice(r * BLOCK, (r + 1) * BLOCK)
            total = (
                term[0, core, at, cols].astype(F32)
                + rv_n[0, at, cols].astype(F32)
                + rv_n[1, at, cols].astype(F32)
            )
            fin[r, :, cols] = (total * md[2, pl.ds(clips[r], 1), cols]).astype(BF16)

        def stage_back(t, carry):
            st_e[t, :, cols] = fin[ranks[t], :, cols]
            return carry

        lax.fori_loop(0, NSEQ, stage_back, 0)
        for k in range(PEERS):
            send_e(c, k).start()
        rv_e[me, :, cols] = st_e[me, :, cols]

    for t in range(ND + max(LAG_D)):
        if t < ND:
            out_project(t)
        for lag, step in zip(LAG_D, (pair_sum, relay, finish), strict=True):
            if lag <= t < ND + lag:
                step(t - lag)

    for c, cols in enumerate(BACK):
        arrived(rv_e.at[0:PEERS, :, cols], rs_e.at[c])
        wide = slice(0, cols.stop - cols.start)
        outbox[:, :, wide] = rv_e[:, :, cols]
        for j in range(BLK_DEV):
            at = slice(j * BLOCK, (j + 1) * BLOCK)
            back = outbox[targets[j], :, wide].astype(F32)
            out[at, cols] = (tok[at, cols].astype(F32) + back).astype(BF16)

    for c, cols in enumerate(COLS):
        left(st_a.at[0:PEERS, :, cols], ss_a.at[c])
        left(gath.at[0:3, 0, :, cols], ss_b.at[c, 0])
        left(gath.at[:, 0, :, cols], ss_b.at[c, 1])
    for c, cols in enumerate(BACK):
        left(st_e.at[0:PEERS, :, cols], ss_e.at[c])
        left(term.at[0:3, 0, :, cols], ss_d.at[c, 0])
        left(term.at[:, 0, :, cols], ss_d.at[c, 1])


def body(
    tokens, block_target, clip_within, modulation,
    inner_attention, inner_hidden, outer_attention, outer_hidden,
):
    smem = pl.BlockSpec(memory_space=pltpu.SMEM)
    vmem = pl.BlockSpec(memory_space=pltpu.VMEM)
    anywhere = pl.BlockSpec(memory_space=pl.ANY)
    dma = pltpu.SemaphoreType.DMA
    return pl.pallas_call(
        kernel,
        out_shape=jax.ShapeDtypeStruct((BLK_DEV * BLOCK, D), BF16),
        in_specs=[smem, smem, vmem, vmem, anywhere, anywhere, anywhere, anywhere],
        out_specs=vmem,
        scratch_shapes=[
            pltpu.VMEM((BLK_DEV, BLOCK, D), BF16),
            pltpu.VMEM((NSEQ, BLOCK, 128 * max(FIRST)), BF16),
            pltpu.VMEM((NSEQ, BLOCK, 128 * max(SECOND)), BF16),
            pltpu.VMEM((NSEQ, BLOCK, D), BF16),
            pltpu.VMEM((NSEQ, BLOCK, D), BF16),
            pltpu.VMEM((Y, 2, ROWS, D), BF16),
            pltpu.VMEM((2, D, HID), BF16),
            pltpu.VMEM((ATT + HID, D), BF16),
            pltpu.VMEM((2, ALL, HID), F32),
            pltpu.VMEM((2, ALL, 2 * HD), BF16),
            pltpu.VMEM((2, ALL, 2 * HD), BF16),
            pltpu.VMEM((2, ALL, 2 * HD), BF16),
            pltpu.VMEM((Y, 2, ROWS, ATT + HID), BF16),
            pltpu.VMEM((Y, 2, ROWS, D), BF16),
            pltpu.VMEM((Y, ROWS, D), BF16),
            pltpu.VMEM((2, HALF, D), BF16),
            pltpu.VMEM((2, ROWS, D), BF16),
            pltpu.VMEM((RCAP, BLOCK, D), BF16),
            pltpu.VMEM((NSEQ, BLOCK, D), BF16),
            pltpu.VMEM((NSEQ, BLOCK, D), BF16),
            pltpu.SMEM((NSEQ,), jnp.int32),
            pltpu.SMEM((RCAP,), jnp.int32),
            pltpu.SMEM((RCAP,), jnp.int32),
            dma((6,)),
            dma((NC,)), dma((NC,)),
            dma((NC, 2)), dma((NC, Y - 1)), dma((NC, 2)),
            dma((ND, 2)), dma((ND,)), dma((ND, 2)), dma((ND,)),
            dma((ND,)), dma((ND,)),
        ],
        compiler_params=pltpu.CompilerParams(
            collective_id=0, has_side_effects=True, vmem_limit_bytes=62 << 20
        ),
        cost_estimate=pl.CostEstimate(
            flops=13_000_000_000, bytes_accessed=17_000_000, transcendentals=2_000_000
        ),
    )(
        block_target, clip_within, tokens, jnp.transpose(modulation, (1, 0, 2)),
        jnp.transpose(inner_attention, (1, 0, 2)), inner_hidden, outer_attention, outer_hidden,
    )


def solution(mesh):
    placed = (
        P(("seq", "head"), None),
        P(),
        P(),
        P("seq", None, None),
        P(None, None, "head"),
        P(None, "head"),
        P("head", None),
        P("head", None),
    )
    return jax.shard_map(
        body, mesh=mesh, in_specs=placed, out_specs=P(("seq", "head"), None), check_vma=False
    )
```
